32 devices in a mesh: rad: 2 (over y), az: 16 (over z, x, core).
Axes of the slice: x: 2, y: 2, z: 4, core: 2. Of those that a mesh axis runs over, the one named last changes fastest.
Arguments:
- dust_density: float32 [128, 256, 128], P('rad', 'az'), may hold values from 0.05 to 1
- dust_velocity: float32 [128, 256, 2, 128], P('rad', 'az'), may hold values from -6 to 6
- gas_density: float32 [256, 1024], P('rad', 'az'), may hold values from 0.5 to 2
- gas_velocity: float32 [256, 2, 1024], P('rad', None, 'az'), may hold values from -6 to 6
- kernel: float32 [128, 128], replicated, may hold values from 0.0005 to 0.005
- grain_param: float32 [128], replicated, may hold values from 0.1 to 10
- cycle_shifts: int32 [128], P('rad'), may hold values from 0 to 255
- fragment_bins: int32 [128, 128], replicated, may hold values from 0 to 127
- gas_map: int32 [128], P('rad'), may hold values from 0 to 255, as said below
Outputs:
- dust_density_out: float32 [128, 256, 128], P('rad', 'az')
- dust_velocity_out: float32 [128, 256, 2, 128], P('rad', 'az')
- gas_velocity_out: float32 [256, 2, 1024], P('rad', None, 'az')
The draws below stay inside these ranges and needn't reach their ends.
Inputs may be any that keep to these rules, and one draw needn't show every extreme that they name: gas_map never decreases along the dust cycles; the first dust cycle maps to gas cycle 0 and the last to gas cycle 256 - 1. `gas_map`: the dust cycles of index i of rad map into gas cycles of index i - 1 or i of rad, and each index after the first has a dust cycle in the gas cycles of index i - 1.
All inputs are finite; a program needn't handle non-finite values.
Results may differ from the reference program's by a relative error of at most 0.000064.
Values sent between devices are 32-bit elements; how exact they have to be, the bound alone decides.
A program may use at most 64 MiB of HBM per device.

```python
import math
import jax
import jax.numpy as jnp
from jax import lax

NB = 128
RD = 64
GR = 128
NRD = 128
NPHI = 256
NRG = 256
NGP = 1024


def draw_gas_map(key, part):
    radial_count = NRD // RD
    steps = jax.random.randint(jax.random.fold_in(key, 11), (radial_count, RD), 1, 8, dtype=jnp.int32)
    before = jnp.cumsum(steps, axis=1) - steps
    total = jnp.maximum(before[:, -1:], 1)
    index = jnp.arange(radial_count, dtype=jnp.int32)
    starts = jnp.where(index == 0, 0, index * GR - GR // 2).astype(jnp.int32)
    ends = jnp.where(index == radial_count - 1, NRG - 1, (index + 1) * GR - GR // 2).astype(jnp.int32)
    mapped = starts[:, None] + before * (ends - starts)[:, None] // total
    return mapped.reshape(NRD).astype(jnp.int32)


def with_ends(entries, rng, smallest, high):
    index_at = [jax.random.randint(jax.random.fold_in(rng, axis), (), 0, length) for axis, length in enumerate(entries.shape)]
    main_axis = entries.shape.index(max(entries.shape))
    beside = index_at[:main_axis] + [(index_at[main_axis] + 1) % entries.shape[main_axis]] + index_at[main_axis + 1:]
    return entries.at[tuple(index_at)].set(smallest).at[tuple(beside)].set(high)


def level_of(own_key, dims, shards, least, largest):
    def one(position, shards_of):
        steps = jax.random.uniform(jax.random.fold_in(jax.random.fold_in(own_key, 6), position), (shards_of,), jnp.float32, least / len(shards), largest / len(shards))
        return jnp.repeat(jnp.exp(steps), dims[position] // shards_of).reshape((-1,) + (1,) * (len(dims) - position - 1))

    level = one(*shards[0])
    for cut in shards[1:]:
        level = level * one(*cut)
    return level


def noise(key, shape, scale, most, split=(), kind=jnp.bfloat16):
    loudness = level_of(key, shape, split, -0.22, 0.18) if split else 1.0
    array = jax.random.normal(key, shape, jnp.float32) * scale * loudness
    return jnp.minimum(jnp.maximum(array, -most), most).astype(kind)


def setup_inputs(seed: int = 0) -> dict:
    splits = jax.random.split(jax.random.key(seed), 10)
    return {
        "dust_density": jnp.clip(jnp.exp(math.log(1.0) - 2.9957323 * jax.random.uniform(splits[0], (NRD, NPHI, NB), jnp.float32) ** level_of(splits[0], (NRD, NPHI, NB), ((0, 2), (1, 16)), -0.2, 0.2)), 0.05, 1.0),
        "dust_velocity": noise(splits[1], (NRD, NPHI, 2, NB), 1.0, 6.0, ((0, 2), (1, 16)), jnp.float32),
        "gas_density": jnp.clip(jnp.exp(math.log(2.0) - 1.3862944 * jax.random.uniform(splits[2], (NRG, NGP), jnp.float32) ** level_of(splits[2], (NRG, NGP), ((0, 2), (1, 16)), -0.2, 0.2)), 0.5, 2.0),
        "gas_velocity": noise(splits[3], (NRG, 2, NGP), 1.0, 6.0, ((0, 2), (2, 16)), jnp.float32),
        "kernel": jnp.clip(jnp.exp(jax.random.uniform(splits[4], (NB, NB), jnp.float32, math.log(0.0005), math.log(0.005))), 0.0005, 0.005),
        "grain_param": jnp.clip(jnp.exp(jax.random.uniform(splits[5], (NB,), jnp.float32, math.log(0.1), math.log(10.0))), 0.1, 10.0),
        "cycle_shifts": with_ends(jax.random.randint(splits[6], (NRD,), 0, NPHI), jax.random.fold_in(splits[6], 1), 0, NPHI - 1).astype(jnp.int32),
        "fragment_bins": with_ends(jax.random.randint(splits[7], (NB, NB), 0, NB), jax.random.fold_in(splits[7], 1), 0, NB - 1).astype(jnp.int32),
        "gas_map": draw_gas_map(jax.random.fold_in(splits[9], 71), 0),
    }


def reference(dust_density, dust_velocity, gas_density, gas_velocity, kernel, grain_param, cycle_shifts, fragment_bins, gas_map):
    nrd, nphi, nb = dust_density.shape
    nrg = gas_density.shape[0]
    index = ((jnp.arange(nphi, dtype=jnp.int32)[None, :] - cycle_shifts[:, None]) % nphi).astype(jnp.int32)
    moved_density = jnp.take_along_axis(dust_density, index[:, :, None], axis=1)
    moved_velocity = jnp.take_along_axis(dust_velocity, index[:, :, None, None], axis=1)
    onehot = (fragment_bins.reshape(-1)[:, None] == jnp.arange(nb, dtype=jnp.int32)[None, :]).astype(jnp.float32)
    table = kernel.reshape(-1)[:, None] * onehot
    cells = nrd * nphi
    block = math.gcd(cells, 1024)

    def coag_block(dens):
        pairs = (dens[:, :, None] * dens[:, None, :]).reshape(dens.shape[0], -1)
        gain = jnp.dot(pairs, table, precision=lax.Precision.HIGHEST)
        loss = dens * jnp.dot(dens, kernel.T, precision=lax.Precision.HIGHEST)
        return dens + gain - loss

    coag_density = lax.map(coag_block, moved_density.reshape(cells // block, block, nb)).reshape(nrd, nphi, nb)
    coarse_density = gas_density.reshape(nrg, nphi, 4).mean(-1)
    coarse_velocity = gas_velocity.reshape(nrg, 2, nphi, 4).mean(-1)
    rho_dust = coarse_density[gas_map]
    u_dust = jnp.transpose(coarse_velocity[gas_map], (0, 2, 1))
    frac = 1.0 - jnp.exp(-rho_dust[:, :, None] / grain_param[None, None, :])
    velocity_out = moved_velocity + (u_dust[:, :, :, None] - moved_velocity) * frac[:, :, None, :]
    momentum = jnp.sum(coag_density[:, :, None, :] * (velocity_out - moved_velocity), axis=3) / nb
    kick = jax.ops.segment_sum(momentum, gas_map, nrg)
    kick = jnp.repeat(jnp.transpose(kick, (0, 2, 1)), 4, axis=2)
    gas_out = gas_velocity - kick / gas_density[:, None, :]
    return coag_density, velocity_out, gas_out
```

```python
import functools

import jax
import jax.numpy as jnp
from jax import lax
from jax.experimental import pallas as pl
from jax.experimental.pallas import tpu as pltpu
from jax.sharding import PartitionSpec as P

F32 = jnp.float32
BF16 = jnp.bfloat16
VMEM = pl.BlockSpec(memory_space=pltpu.VMEM)
SMEM = pl.BlockSpec(memory_space=pltpu.SMEM)
GROUP = 6
ABT = (((1,), (1,)), ((), ()))


def split_parts(x):
    hi = x.astype(BF16)
    return hi, (x - hi.astype(F32)).astype(BF16)


def diagonals(x):
    n = x.shape[0]
    lane = lax.broadcasted_iota(jnp.int32, x.shape, 1)
    step = 1
    while step < n:
        x = jnp.where((lane & step) != 0, pltpu.roll(x, n - step, 0), x)
        step *= 2
    return x


def coag_kernel(dens_ref, rate_ref, bins_ref, out_ref, rates, places, acc):
    n = rate_ref.shape[0]
    half = n // 2
    rate = rate_ref[...]
    place = bins_ref[...].astype(F32)
    dist = lax.broadcasted_iota(jnp.int32, (n, n), 0)
    rates[0] = jnp.where(dist <= half, diagonals(rate.T), 0.0)
    rates[1] = jnp.where((dist > 0) & (dist < half), diagonals(rate), 0.0)
    places[0] = diagonals(place.T)
    places[1] = diagonals(place)

    dens = dens_ref[...]
    hi, lo = split_parts(dens)
    rate_hi, rate_lo = split_parts(rate)
    both = jnp.concatenate([rate_hi, rate_lo], axis=0)
    lost = lax.dot_general(
        jnp.concatenate([hi, lo], axis=1),
        jnp.concatenate([both, both], axis=1),
        ABT,
        preferred_element_type=F32,
    )
    out_ref[...] = dens - dens * (lost[:, :n] + lost[:, n:])
    acc[...] = jnp.zeros_like(acc)
    bin_id = lax.broadcasted_iota(jnp.int32, (n, n), 0).astype(F32)

    def step(g, carry):
        table_hi, table_lo, pair_hi, pair_lo = [], [], [], []
        for t in range(GROUP):
            d = g * GROUP + t
            row = pl.ds(d, 1)
            table = jnp.where(bin_id == places[0, row, :], rates[0, row, :], 0.0) + jnp.where(
                bin_id == places[1, row, :], rates[1, row, :], 0.0
            )
            h, l = split_parts(table)
            table_hi.append(h)
            table_lo.append(l)
            x = dens_ref[...]
            h, l = split_parts(x * pltpu.roll(x, n - d, 1))
            pair_hi.append(h)
            pair_lo.append(l)
        table = jnp.concatenate(
            [jnp.concatenate(table_hi, axis=1), jnp.concatenate(table_lo, axis=1)], axis=0
        )
        acc[...] += lax.dot_general(
            jnp.concatenate(pair_hi, axis=1), table, ABT, preferred_element_type=F32
        ) + lax.dot_general(
            jnp.concatenate(pair_lo, axis=1), table, ABT, preferred_element_type=F32
        )
        return carry

    lax.fori_loop(0, -(-(half + 1) // GROUP), step, 0)
    out_ref[...] += acc[:, :n] + acc[:, n:]


def coagulate(dens, kernel, fragment_bins):
    cells, n = dens.shape
    return pl.pallas_call(
        coag_kernel,
        out_shape=jax.ShapeDtypeStruct((cells, n), F32),
        in_specs=[VMEM, VMEM, VMEM],
        out_specs=VMEM,
        scratch_shapes=[
            pltpu.VMEM((2, n, n), F32),
            pltpu.VMEM((2, n, n), F32),
            pltpu.VMEM((cells, 2 * n), F32),
        ],
        compiler_params=pltpu.CompilerParams(vmem_limit_bytes=48 * 2**20),
        cost_estimate=pl.CostEstimate(
            flops=4 * cells * n * n * n, bytes_accessed=8 * cells * n, transcendentals=0
        ),
        name="coagulate",
    )(dens, kernel, fragment_bins)


def turn_kernel(owned, per_cell, shifts_ref, x_ref, out_ref, twice):
    parts, _, rows, n = x_ref.shape
    whole = parts * rows
    first = lax.axis_index("az") * owned
    for c in range(owned):
        x = x_ref[:, c].reshape(whole, n)
        twice[c, :whole] = x
        twice[c, whole:] = x
        shift = shifts_ref[first + c] * per_cell
        out_ref[:, c] = twice[c, pl.ds(whole - shift, whole), :].reshape(parts, rows, n)


def turn(x, shifts, per_cell):
    parts, owned, rows, n = x.shape
    return pl.pallas_call(
        functools.partial(turn_kernel, owned, per_cell),
        out_shape=jax.ShapeDtypeStruct(x.shape, F32),
        in_specs=[SMEM, VMEM],
        out_specs=VMEM,
        scratch_shapes=[pltpu.VMEM((owned, 2 * parts * rows, n), F32)],
        compiler_params=pltpu.CompilerParams(vmem_limit_bytes=32 * 2**20),
        cost_estimate=pl.CostEstimate(flops=0, bytes_accessed=8 * x.size, transcendentals=0),
        name="turn",
    )(shifts, x)


def coarse_kernel(dens_ref, vel_ref, out_ref):
    fine = dens_ref.shape[1]
    cells = fine // 4
    q = lax.broadcasted_iota(jnp.int32, (fine, cells), 0)
    p = lax.broadcasted_iota(jnp.int32, (fine, cells), 1)
    pool = jnp.where(q // 4 == p, 0.25, 0.0)
    vel = vel_ref[...]
    parts = [dens_ref[...], vel[:, :fine], vel[:, fine:]]
    for i, x in enumerate(parts):
        out_ref[:, i * cells : (i + 1) * cells] = jnp.dot(
            x, pool, precision=lax.Precision.HIGHEST, preferred_element_type=F32
        )


def drag_kernel(
    map_ref, prev_ref, own_ref, grain_ref, coag_ref, vel_ref, vel_out_ref, back_ref, kick_ref
):
    cycles = map_ref.shape[1]
    gas_cycles = own_ref.shape[0]
    cells = own_ref.shape[1] // 3
    n = grain_ref.shape[1]
    first = (lax.axis_index("rad") - 1) * gas_cycles
    row = lax.broadcasted_iota(jnp.int32, (2 * gas_cycles, cycles), 0)
    select = jnp.where(map_ref[...] - first == row, 1.0, 0.0)
    near = jnp.concatenate([prev_ref[...], own_ref[...]], axis=0)
    gas = lax.dot_general(
        near.T, select, (((1,), (0,)), ((), ())),
        precision=lax.Precision.HIGHEST, preferred_element_type=F32,
    )
    grain = grain_ref[...]
    lane = lax.broadcasted_iota(jnp.int32, (cells, cycles), 1)
    moment = [jnp.zeros((cells, cycles), F32) for _ in range(2)]
    for r in range(cycles):
        rho = gas[:cells, r : r + 1]
        frac = 1.0 - jnp.exp(-rho / grain)
        dens = coag_ref[r * cells : (r + 1) * cells, :]
        for c in range(2):
            u = gas[(c + 1) * cells : (c + 2) * cells, r : r + 1]
            rows = pl.ds(r * 2 * cells + c, cells, 2)
            v = vel_ref[rows, :]
            new = v + (u - v) * frac
            vel_out_ref[rows, :] = new
            m = jnp.sum(dens * (new - v), axis=1, keepdims=True)
            moment[c] = jnp.where(lane == r, m, moment[c])
    both = jnp.concatenate(moment, axis=0) / n
    kick = lax.dot_general(
        both, select, ABT, precision=lax.Precision.HIGHEST, preferred_element_type=F32
    )
    back_ref[...] = kick[:, :gas_cycles]
    kick_ref[...] = kick[:, gas_cycles:]


def gas_kernel(kick_ref, from_next_ref, dens_ref, vel_ref, out_ref):
    fine = dens_ref.shape[1]
    cells = fine // 4
    kick = (kick_ref[...] + from_next_ref[...]).T
    p = lax.broadcasted_iota(jnp.int32, (cells, fine), 0)
    q = lax.broadcasted_iota(jnp.int32, (cells, fine), 1)
    spread = jnp.where(q // 4 == p, 1.0, 0.0)
    dens = dens_ref[...]
    for c in range(2):
        wide = jnp.dot(
            kick[:, c * cells : (c + 1) * cells], spread,
            precision=lax.Precision.HIGHEST, preferred_element_type=F32,
        )
        own = slice(c * fine, (c + 1) * fine)
        out_ref[:, own] = vel_ref[:, own] - wide / dens


def shifted(block, axis, distance):
    devices = range(lax.axis_size(axis))
    route = [(i - distance, i) for i in devices if i - distance in devices]
    return lax.ppermute(block, axis, route)


def exchange(x):
    return lax.all_to_all(x, "az", split_axis=0, concat_axis=0, tiled=True)


def body(
    dust_density,
    dust_velocity,
    gas_density,
    gas_velocity,
    kernel,
    grain_param,
    cycle_shifts,
    fragment_bins,
    gas_map,
):
    cycles, cells, bins = dust_density.shape
    gas_cycles, fine = gas_density.shape
    parts = lax.axis_size("az")
    owned = cycles // parts
    gas_flat = gas_velocity.reshape(gas_cycles, 2 * fine)

    vel = exchange(dust_velocity.reshape(parts, owned, 2 * cells, bins))
    coag = coagulate(dust_density.reshape(cycles * cells, bins), kernel, fragment_bins)
    coag = exchange(coag.reshape(parts, owned, cells, bins))
    vel = exchange(turn(vel, cycle_shifts, 2))
    coag = exchange(turn(coag, cycle_shifts, 1))

    coarse = pl.pallas_call(
        coarse_kernel,
        out_shape=jax.ShapeDtypeStruct((gas_cycles, 3 * cells), F32),
        name="coarse",
    )(gas_density, gas_flat)
    prev = shifted(coarse, "rad", 1)

    coag = coag.reshape(cycles * cells, bins)
    vel_out, back, kick = pl.pallas_call(
        drag_kernel,
        out_shape=(
            jax.ShapeDtypeStruct((2 * cycles * cells, bins), F32),
            jax.ShapeDtypeStruct((2 * cells, gas_cycles), F32),
            jax.ShapeDtypeStruct((2 * cells, gas_cycles), F32),
        ),
        compiler_params=pltpu.CompilerParams(vmem_limit_bytes=32 * 2**20),
        name="drag",
    )(
        gas_map.reshape(1, cycles),
        prev,
        coarse,
        grain_param.reshape(1, bins),
        coag,
        vel.reshape(2 * cycles * cells, bins),
    )
    from_next = shifted(back, "rad", -1)
    gas_out = pl.pallas_call(
        gas_kernel,
        out_shape=jax.ShapeDtypeStruct((gas_cycles, 2 * fine), F32),
        name="gas",
    )(kick, from_next, gas_density, gas_flat)
    return (
        coag.reshape(cycles, cells, bins),
        vel_out.reshape(cycles, cells, 2, bins),
        gas_out.reshape(gas_cycles, 2, fine),
    )


def solution(mesh):
    placed = (
        P("rad", "az", None),
        P("rad", "az", None, None),
        P("rad", "az"),
        P("rad", None, "az"),
        P(),
        P(),
        P("rad"),
        P(),
        P("rad"),
    )
    return jax.shard_map(
        body,
        mesh=mesh,
        in_specs=placed,
        out_specs=(P("rad", "az", None), P("rad", "az", None, None), P("rad", None, "az")),
        check_vma=False,
    )
```

```python
import functools

import jax
import jax.numpy as jnp
from jax import lax
from jax.experimental import pallas as pl
from jax.experimental.pallas import tpu as pltpu
from jax.sharding import PartitionSpec as P

F32 = jnp.float32
BF16 = jnp.bfloat16
VMEM = pl.BlockSpec(memory_space=pltpu.VMEM)
SMEM = pl.BlockSpec(memory_space=pltpu.SMEM)
GROUP = 6
ABT = (((1,), (1,)), ((), ()))


def split_parts(x):
    hi = x.astype(BF16)
    return hi, (x - hi.astype(F32)).astype(BF16)


def diagonals(x):
    n = x.shape[0]
    lane = lax.broadcasted_iota(jnp.int32, x.shape, 1)
    step = 1
    while step < n:
        x = jnp.where((lane & step) != 0, pltpu.roll(x, n - step, 0), x)
        step *= 2
    return x


def coag_kernel(dens_ref, rate_ref, bins_ref, out_ref, rates, places, acc):
    n = rate_ref.shape[0]
    half = n // 2
    rate = rate_ref[...]
    place = bins_ref[...].astype(F32)
    dist = lax.broadcasted_iota(jnp.int32, (n, n), 0)
    rates[0] = jnp.where(dist <= half, diagonals(rate.T), 0.0)
    rates[1] = jnp.where((dist > 0) & (dist < half), diagonals(rate), 0.0)
    places[0] = diagonals(place.T)
    places[1] = diagonals(place)

    dens = dens_ref[...]
    hi, lo = split_parts(dens)
    rate_hi, rate_lo = split_parts(rate)
    both = jnp.concatenate([rate_hi, rate_lo], axis=0)
    lost = lax.dot_general(
        jnp.concatenate([hi, lo], axis=1),
        jnp.concatenate([both, both], axis=1),
        ABT,
        preferred_element_type=F32,
    )
    out_ref[...] = dens - dens * (lost[:, :n] + lost[:, n:])
    acc[...] = jnp.zeros_like(acc)
    bin_id = lax.broadcasted_iota(jnp.int32, (n, n), 0).astype(F32)

    def step(g, carry):
        table_hi, table_lo, pair_hi, pair_lo = [], [], [], []
        for t in range(GROUP):
            d = g * GROUP + t
            row = pl.ds(d, 1)
            table = jnp.where(bin_id == places[0, row, :], rates[0, row, :], 0.0) + jnp.where(
                bin_id == places[1, row, :], rates[1, row, :], 0.0
            )
            h, l = split_parts(table)
            table_hi.append(h)
            table_lo.append(l)
            x = dens_ref[...]
            h, l = split_parts(x * pltpu.roll(x, n - d, 1))
            pair_hi.append(h)
            pair_lo.append(l)
        table = jnp.concatenate(
            [jnp.concatenate(table_hi, axis=1), jnp.concatenate(table_lo, axis=1)], axis=0
        )
        acc[...] += lax.dot_general(
            jnp.concatenate(pair_hi, axis=1), table, ABT, preferred_element_type=F32
        ) + lax.dot_general(
            jnp.concatenate(pair_lo, axis=1), table, ABT, preferred_element_type=F32
        )
        return carry

    lax.fori_loop(0, -(-(half + 1) // GROUP), step, 0)
    out_ref[...] += acc[:, :n] + acc[:, n:]


def coagulate(dens, kernel, fragment_bins):
    cells, n = dens.shape
    return pl.pallas_call(
        coag_kernel,
        out_shape=jax.ShapeDtypeStruct((cells, n), F32),
        in_specs=[VMEM, VMEM, VMEM],
        out_specs=VMEM,
        scratch_shapes=[
            pltpu.VMEM((2, n, n), F32),
            pltpu.VMEM((2, n, n), F32),
            pltpu.VMEM((cells, 2 * n), F32),
        ],
        compiler_params=pltpu.CompilerParams(vmem_limit_bytes=48 * 2**20),
        cost_estimate=pl.CostEstimate(
            flops=4 * cells * n * n * n, bytes_accessed=8 * cells * n, transcendentals=0
        ),
        name="coagulate",
    )(dens, kernel, fragment_bins)


def move_kernel(
    owned, shifts_ref, vel_ref, dens_ref, vel_out, dens_out,
    vel_land, dens_land, vel_turned, dens_turned, vel_twice, dens_twice, send_sem, recv_sem,
):
    me = lax.axis_index("az")
    parts = vel_ref.shape[0]
    half = owned // 2
    vel = (vel_ref, vel_land, vel_turned, vel_out, vel_twice, 2)
    dens = (dens_ref, dens_land, dens_turned, dens_out, dens_twice, 1)
    units = [vel + (0, half), vel + (half, owned - half), dens + (0, owned)]

    barrier = pltpu.get_barrier_semaphore()

    def greet(k, carry):
        other = lax.rem(me + k, parts)
        pl.semaphore_signal(
            barrier, inc=1, device_id={"az": other}, device_id_type=pl.DeviceIdType.MESH
        )
        return carry

    lax.fori_loop(1, parts, greet, 0)
    pl.semaphore_wait(barrier, parts - 1)

    def copy(phase, u, k):
        source, land, turned, end, _, _, first, count = units[u]
        src, dst = (source, land) if phase == 0 else (turned, end)
        other = lax.rem(me + k, parts)
        own = pl.ds(first, count)
        return pltpu.make_async_remote_copy(
            src_ref=src.at[other, own],
            dst_ref=dst.at[me, own],
            send_sem=send_sem.at[phase, u, k],
            recv_sem=recv_sem.at[phase, u, k],
            device_id={"az": other},
            device_id_type=pl.DeviceIdType.MESH,
        )

    def each(act):
        def step(k, carry):
            act(k)
            return carry

        lax.fori_loop(1, parts, step, 0)

    for u, (source, land, _, _, _, _, first, count) in enumerate(units):
        each(lambda k: copy(0, u, k).start())
        land[me, pl.ds(first, count)] = source[me, pl.ds(first, count)]

    for u, (_, land, turned, end, twice, per_cell, first, count) in enumerate(units):
        each(lambda k: copy(0, u, k).wait_recv())
        rows, n = land.shape[2:]
        whole = parts * rows
        for c in range(first, first + count):
            x = land[:, c].reshape(whole, n)
            twice[c, :whole] = x
            twice[c, whole:] = x
            shift = shifts_ref[me * owned + c] * per_cell
            turned[:, c] = twice[c, pl.ds(whole - shift, whole), :].reshape(parts, rows, n)
        each(lambda k: copy(1, u, k).start())
        end[me, pl.ds(first, count)] = turned[me, pl.ds(first, count)]

    for u in range(len(units)):
        each(lambda k: copy(1, u, k).wait_recv())
    for phase in range(2):
        for u in range(len(units)):
            each(lambda k: copy(phase, u, k).wait_send())


def move(vel, dens, shifts):
    parts, owned, rows, n = vel.shape
    cells = dens.shape[2]
    return pl.pallas_call(
        functools.partial(move_kernel, owned),
        out_shape=(
            jax.ShapeDtypeStruct(vel.shape, F32),
            jax.ShapeDtypeStruct(dens.shape, F32),
        ),
        in_specs=[SMEM, VMEM, VMEM],
        out_specs=(VMEM, VMEM),
        scratch_shapes=[
            pltpu.VMEM(vel.shape, F32),
            pltpu.VMEM(dens.shape, F32),
            pltpu.VMEM(vel.shape, F32),
            pltpu.VMEM(dens.shape, F32),
            pltpu.VMEM((owned, 2 * parts * rows, n), F32),
            pltpu.VMEM((owned, 2 * parts * cells, n), F32),
            pltpu.SemaphoreType.DMA((2, 3, parts)),
            pltpu.SemaphoreType.DMA((2, 3, parts)),
        ],
        compiler_params=pltpu.CompilerParams(
            collective_id=0, has_side_effects=True, vmem_limit_bytes=40 * 2**20
        ),
        cost_estimate=pl.CostEstimate(
            flops=0, bytes_accessed=8 * (vel.size + dens.size), transcendentals=0
        ),
        name="move",
    )(shifts, vel, dens)


def coarse_kernel(dens_ref, vel_ref, out_ref):
    fine = dens_ref.shape[1]
    cells = fine // 4
    q = lax.broadcasted_iota(jnp.int32, (fine, cells), 0)
    p = lax.broadcasted_iota(jnp.int32, (fine, cells), 1)
    pool = jnp.where(q // 4 == p, 0.25, 0.0)
    vel = vel_ref[...]
    parts = [dens_ref[...], vel[:, :fine], vel[:, fine:]]
    for i, x in enumerate(parts):
        out_ref[:, i * cells : (i + 1) * cells] = jnp.dot(
            x, pool, precision=lax.Precision.HIGHEST, preferred_element_type=F32
        )


def drag_kernel(
    map_ref, prev_ref, own_ref, grain_ref, coag_ref, vel_ref, vel_out_ref, back_ref, kick_ref
):
    cycles = map_ref.shape[1]
    gas_cycles = own_ref.shape[0]
    cells = own_ref.shape[1] // 3
    n = grain_ref.shape[1]
    first = (lax.axis_index("rad") - 1) * gas_cycles
    row = lax.broadcasted_iota(jnp.int32, (2 * gas_cycles, cycles), 0)
    select = jnp.where(map_ref[...] - first == row, 1.0, 0.0)
    near = jnp.concatenate([prev_ref[...], own_ref[...]], axis=0)
    gas = lax.dot_general(
        near.T, select, (((1,), (0,)), ((), ())),
        precision=lax.Precision.HIGHEST, preferred_element_type=F32,
    )
    grain = grain_ref[...]
    lane = lax.broadcasted_iota(jnp.int32, (cells, cycles), 1)
    moment = [jnp.zeros((cells, cycles), F32) for _ in range(2)]
    for r in range(cycles):
        rho = gas[:cells, r : r + 1]
        frac = 1.0 - jnp.exp(-rho / grain)
        dens = coag_ref[r * cells : (r + 1) * cells, :]
        for c in range(2):
            u = gas[(c + 1) * cells : (c + 2) * cells, r : r + 1]
            rows = pl.ds(r * 2 * cells + c, cells, 2)
            v = vel_ref[rows, :]
            new = v + (u - v) * frac
            vel_out_ref[rows, :] = new
            m = jnp.sum(dens * (new - v), axis=1, keepdims=True)
            moment[c] = jnp.where(lane == r, m, moment[c])
    both = jnp.concatenate(moment, axis=0) / n
    kick = lax.dot_general(
        both, select, ABT, precision=lax.Precision.HIGHEST, preferred_element_type=F32
    )
    back_ref[...] = kick[:, :gas_cycles]
    kick_ref[...] = kick[:, gas_cycles:]


def gas_kernel(kick_ref, from_next_ref, dens_ref, vel_ref, out_ref):
    fine = dens_ref.shape[1]
    cells = fine // 4
    kick = (kick_ref[...] + from_next_ref[...]).T
    p = lax.broadcasted_iota(jnp.int32, (cells, fine), 0)
    q = lax.broadcasted_iota(jnp.int32, (cells, fine), 1)
    spread = jnp.where(q // 4 == p, 1.0, 0.0)
    dens = dens_ref[...]
    for c in range(2):
        wide = jnp.dot(
            kick[:, c * cells : (c + 1) * cells], spread,
            precision=lax.Precision.HIGHEST, preferred_element_type=F32,
        )
        own = slice(c * fine, (c + 1) * fine)
        out_ref[:, own] = vel_ref[:, own] - wide / dens


def shifted(block, axis, distance):
    devices = range(lax.axis_size(axis))
    route = [(i - distance, i) for i in devices if i - distance in devices]
    return lax.ppermute(block, axis, route)


def body(
    dust_density,
    dust_velocity,
    gas_density,
    gas_velocity,
    kernel,
    grain_param,
    cycle_shifts,
    fragment_bins,
    gas_map,
):
    cycles, cells, bins = dust_density.shape
    gas_cycles, fine = gas_density.shape
    parts = lax.axis_size("az")
    owned = cycles // parts
    gas_flat = gas_velocity.reshape(gas_cycles, 2 * fine)

    coag = coagulate(dust_density.reshape(cycles * cells, bins), kernel, fragment_bins)
    vel, coag = move(
        dust_velocity.reshape(parts, owned, 2 * cells, bins),
        coag.reshape(parts, owned, cells, bins),
        cycle_shifts,
    )

    coarse = pl.pallas_call(
        coarse_kernel,
        out_shape=jax.ShapeDtypeStruct((gas_cycles, 3 * cells), F32),
        name="coarse",
    )(gas_density, gas_flat)
    prev = shifted(coarse, "rad", 1)

    coag = coag.reshape(cycles * cells, bins)
    vel_out, back, kick = pl.pallas_call(
        drag_kernel,
        out_shape=(
            jax.ShapeDtypeStruct((2 * cycles * cells, bins), F32),
            jax.ShapeDtypeStruct((2 * cells, gas_cycles), F32),
            jax.ShapeDtypeStruct((2 * cells, gas_cycles), F32),
        ),
        compiler_params=pltpu.CompilerParams(vmem_limit_bytes=32 * 2**20),
        name="drag",
    )(
        gas_map.reshape(1, cycles),
        prev,
        coarse,
        grain_param.reshape(1, bins),
        coag,
        vel.reshape(2 * cycles * cells, bins),
    )
    from_next = shifted(back, "rad", -1)
    gas_out = pl.pallas_call(
        gas_kernel,
        out_shape=jax.ShapeDtypeStruct((gas_cycles, 2 * fine), F32),
        name="gas",
    )(kick, from_next, gas_density, gas_flat)
    return (
        coag.reshape(cycles, cells, bins),
        vel_out.reshape(cycles, cells, 2, bins),
        gas_out.reshape(gas_cycles, 2, fine),
    )


def solution(mesh):
    placed = (
        P("rad", "az", None),
        P("rad", "az", None, None),
        P("rad", "az"),
        P("rad", None, "az"),
        P(),
        P(),
        P("rad"),
        P(),
        P("rad"),
    )
    return jax.shard_map(
        body,
        mesh=mesh,
        in_specs=placed,
        out_specs=(P("rad", "az", None), P("rad", "az", None, None), P("rad", None, "az")),
        check_vma=False,
    )
```

```python
import functools

import jax
import jax.numpy as jnp
from jax import lax
from jax.experimental import pallas as pl
from jax.experimental.pallas import tpu as pltpu
from jax.sharding import PartitionSpec as P

F32 = jnp.float32
BF16 = jnp.bfloat16
VMEM = pl.BlockSpec(memory_space=pltpu.VMEM)
SMEM = pl.BlockSpec(memory_space=pltpu.SMEM)
GROUP = 6
ABT = (((1,), (1,)), ((), ()))


def split_parts(x):
    hi = x.astype(BF16)
    return hi, (x - hi.astype(F32)).astype(BF16)


def diagonals(x):
    n = x.shape[0]
    lane = lax.broadcasted_iota(jnp.int32, x.shape, 1)
    step = 1
    while step < n:
        x = jnp.where((lane & step) != 0, pltpu.roll(x, n - step, 0), x)
        step *= 2
    return x


def coagulate(dens_ref, rate_ref, bins_ref, out_ref, rates, places, acc):
    n = rate_ref.shape[0]
    half = n // 2
    rate = rate_ref[...]
    place = bins_ref[...].astype(F32)
    dist = lax.broadcasted_iota(jnp.int32, (n, n), 0)
    rates[0] = jnp.where(dist <= half, diagonals(rate.T), 0.0)
    rates[1] = jnp.where((dist > 0) & (dist < half), diagonals(rate), 0.0)
    places[0] = diagonals(place.T)
    places[1] = diagonals(place)

    dens = dens_ref[...]
    hi, lo = split_parts(dens)
    rate_hi, rate_lo = split_parts(rate)
    both = jnp.concatenate([rate_hi, rate_lo], axis=0)
    lost = lax.dot_general(
        jnp.concatenate([hi, lo], axis=1),
        jnp.concatenate([both, both], axis=1),
        ABT,
        preferred_element_type=F32,
    )
    out_ref[...] = dens - dens * (lost[:, :n] + lost[:, n:])
    acc[...] = jnp.zeros_like(acc)
    bin_id = lax.broadcasted_iota(jnp.int32, (n, n), 0).astype(F32)

    def step(g, carry):
        table_hi, table_lo, pair_hi, pair_lo = [], [], [], []
        for t in range(GROUP):
            d = g * GROUP + t
            row = pl.ds(d, 1)
            table = jnp.where(bin_id == places[0, row, :], rates[0, row, :], 0.0) + jnp.where(
                bin_id == places[1, row, :], rates[1, row, :], 0.0
            )
            h, l = split_parts(table)
            table_hi.append(h)
            table_lo.append(l)
            x = dens_ref[...]
            h, l = split_parts(x * pltpu.roll(x, n - d, 1))
            pair_hi.append(h)
            pair_lo.append(l)
        table = jnp.concatenate(
            [jnp.concatenate(table_hi, axis=1), jnp.concatenate(table_lo, axis=1)], axis=0
        )
        acc[...] += lax.dot_general(
            jnp.concatenate(pair_hi, axis=1), table, ABT, preferred_element_type=F32
        ) + lax.dot_general(
            jnp.concatenate(pair_lo, axis=1), table, ABT, preferred_element_type=F32
        )
        return carry

    lax.fori_loop(0, -(-(half + 1) // GROUP), step, 0)
    out_ref[...] += acc[:, :n] + acc[:, n:]


def move_kernel(
    owned, shifts_ref, vel_ref, start_ref, rate_ref, bins_ref, vel_out, dens_out,
    flat, dens_ref, rates, places, acc, vel_land, dens_land, vel_turned, dens_turned, vel_twice, dens_twice, send_sem, recv_sem,
):
    me = lax.axis_index("az")
    parts = vel_ref.shape[0]
    half = owned // 2
    vel = (vel_ref, vel_land, vel_turned, vel_out, vel_twice, 2)
    dens = (dens_ref, dens_land, dens_turned, dens_out, dens_twice, 1)
    units = [vel + (0, half), vel + (half, owned - half), dens + (0, owned)]

    barrier = pltpu.get_barrier_semaphore()

    def greet(k, carry):
        other = lax.rem(me + k, parts)
        pl.semaphore_signal(
            barrier, inc=1, device_id={"az": other}, device_id_type=pl.DeviceIdType.MESH
        )
        return carry

    lax.fori_loop(1, parts, greet, 0)
    pl.semaphore_wait(barrier, parts - 1)

    def copy(phase, u, k):
        source, land, turned, end, _, _, first, count = units[u]
        src, dst = (source, land) if phase == 0 else (turned, end)
        other = lax.rem(me + k, parts)
        own = pl.ds(first, count)
        return pltpu.make_async_remote_copy(
            src_ref=src.at[other, own],
            dst_ref=dst.at[me, own],
            send_sem=send_sem.at[phase, u, k],
            recv_sem=recv_sem.at[phase, u, k],
            device_id={"az": other},
            device_id_type=pl.DeviceIdType.MESH,
        )

    def each(act):
        def step(k, carry):
            act(k)
            return carry

        lax.fori_loop(1, parts, step, 0)

    for u, (source, land, _, _, _, _, first, count) in enumerate(units):
        if source is dens_ref:
            coagulate(start_ref, rate_ref, bins_ref, flat, rates, places, acc)
            dens_ref[...] = flat[...].reshape(dens_ref.shape)
        each(lambda k: copy(0, u, k).start())
        land[me, pl.ds(first, count)] = source[me, pl.ds(first, count)]

    for u, (_, land, turned, end, twice, per_cell, first, count) in enumerate(units):
        each(lambda k: copy(0, u, k).wait_recv())
        rows, n = land.shape[2:]
        whole = parts * rows
        for c in range(first, first + count):
            x = land[:, c].reshape(whole, n)
            twice[c, :whole] = x
            twice[c, whole:] = x
            shift = shifts_ref[me * owned + c] * per_cell
            turned[:, c] = twice[c, pl.ds(whole - shift, whole), :].reshape(parts, rows, n)
        each(lambda k: copy(1, u, k).start())
        end[me, pl.ds(first, count)] = turned[me, pl.ds(first, count)]

    for u in range(len(units)):
        each(lambda k: copy(1, u, k).wait_recv())
    for phase in range(2):
        for u in range(len(units)):
            each(lambda k: copy(phase, u, k).wait_send())


def move(vel, dens, shifts, kernel, fragment_bins):
    parts, owned, rows, n = vel.shape
    cells = rows // 2
    moved = (parts, owned, cells, n)
    return pl.pallas_call(
        functools.partial(move_kernel, owned),
        out_shape=(
            jax.ShapeDtypeStruct(vel.shape, F32),
            jax.ShapeDtypeStruct(moved, F32),
        ),
        in_specs=[SMEM, VMEM, VMEM, VMEM, VMEM],
        out_specs=(VMEM, VMEM),
        scratch_shapes=[
            pltpu.VMEM(dens.shape, F32),
            pltpu.VMEM(moved, F32),
            pltpu.VMEM((2, n, n), F32),
            pltpu.VMEM((2, n, n), F32),
            pltpu.VMEM((dens.shape[0], 2 * n), F32),
            pltpu.VMEM(vel.shape, F32),
            pltpu.VMEM(moved, F32),
            pltpu.VMEM(vel.shape, F32),
            pltpu.VMEM(moved, F32),
            pltpu.VMEM((owned, 2 * parts * rows, n), F32),
            pltpu.VMEM((owned, 2 * parts * cells, n), F32),
            pltpu.SemaphoreType.DMA((2, 3, parts)),
            pltpu.SemaphoreType.DMA((2, 3, parts)),
        ],
        compiler_params=pltpu.CompilerParams(
            collective_id=0, has_side_effects=True, vmem_limit_bytes=48 * 2**20
        ),
        cost_estimate=pl.CostEstimate(
            flops=4 * dens.size * n * n,
            bytes_accessed=8 * (vel.size + dens.size),
            transcendentals=0,
        ),
        name="move",
    )(shifts, vel, dens, kernel, fragment_bins)


def coarse_kernel(dens_ref, vel_ref, out_ref):
    fine = dens_ref.shape[1]
    cells = fine // 4
    q = lax.broadcasted_iota(jnp.int32, (fine, cells), 0)
    p = lax.broadcasted_iota(jnp.int32, (fine, cells), 1)
    pool = jnp.where(q // 4 == p, 0.25, 0.0)
    vel = vel_ref[...]
    parts = [dens_ref[...], vel[:, :fine], vel[:, fine:]]
    for i, x in enumerate(parts):
        out_ref[:, i * cells : (i + 1) * cells] = jnp.dot(
            x, pool, precision=lax.Precision.HIGHEST, preferred_element_type=F32
        )


def drag_kernel(
    map_ref, prev_ref, own_ref, grain_ref, coag_ref, vel_ref, vel_out_ref, back_ref, kick_ref
):
    cycles = map_ref.shape[1]
    gas_cycles = own_ref.shape[0]
    cells = own_ref.shape[1] // 3
    n = grain_ref.shape[1]
    first = (lax.axis_index("rad") - 1) * gas_cycles
    row = lax.broadcasted_iota(jnp.int32, (2 * gas_cycles, cycles), 0)
    select = jnp.where(map_ref[...] - first == row, 1.0, 0.0)
    near = jnp.concatenate([prev_ref[...], own_ref[...]], axis=0)
    gas = lax.dot_general(
        near.T, select, (((1,), (0,)), ((), ())),
        precision=lax.Precision.HIGHEST, preferred_element_type=F32,
    )
    grain = grain_ref[...]
    lane = lax.broadcasted_iota(jnp.int32, (cells, cycles), 1)
    moment = [jnp.zeros((cells, cycles), F32) for _ in range(2)]
    for r in range(cycles):
        rho = gas[:cells, r : r + 1]
        frac = 1.0 - jnp.exp(-rho / grain)
        dens = coag_ref[r * cells : (r + 1) * cells, :]
        for c in range(2):
            u = gas[(c + 1) * cells : (c + 2) * cells, r : r + 1]
            rows = pl.ds(r * 2 * cells + c, cells, 2)
            v = vel_ref[rows, :]
            new = v + (u - v) * frac
            vel_out_ref[rows, :] = new
            m = jnp.sum(dens * (new - v), axis=1, keepdims=True)
            moment[c] = jnp.where(lane == r, m, moment[c])
    both = jnp.concatenate(moment, axis=0) / n
    kick = lax.dot_general(
        both, select, ABT, precision=lax.Precision.HIGHEST, preferred_element_type=F32
    )
    back_ref[...] = kick[:, :gas_cycles]
    kick_ref[...] = kick[:, gas_cycles:]


def gas_kernel(kick_ref, from_next_ref, dens_ref, vel_ref, out_ref):
    fine = dens_ref.shape[1]
    cells = fine // 4
    kick = (kick_ref[...] + from_next_ref[...]).T
    p = lax.broadcasted_iota(jnp.int32, (cells, fine), 0)
    q = lax.broadcasted_iota(jnp.int32, (cells, fine), 1)
    spread = jnp.where(q // 4 == p, 1.0, 0.0)
    dens = dens_ref[...]
    for c in range(2):
        wide = jnp.dot(
            kick[:, c * cells : (c + 1) * cells], spread,
            precision=lax.Precision.HIGHEST, preferred_element_type=F32,
        )
        own = slice(c * fine, (c + 1) * fine)
        out_ref[:, own] = vel_ref[:, own] - wide / dens


def shifted(block, axis, distance):
    devices = range(lax.axis_size(axis))
    route = [(i - distance, i) for i in devices if i - distance in devices]
    return lax.ppermute(block, axis, route)


def body(
    dust_density,
    dust_velocity,
    gas_density,
    gas_velocity,
    kernel,
    grain_param,
    cycle_shifts,
    fragment_bins,
    gas_map,
):
    cycles, cells, bins = dust_density.shape
    gas_cycles, fine = gas_density.shape
    parts = lax.axis_size("az")
    owned = cycles // parts
    gas_flat = gas_velocity.reshape(gas_cycles, 2 * fine)

    vel, coag = move(
        dust_velocity.reshape(parts, owned, 2 * cells, bins),
        dust_density.reshape(cycles * cells, bins),
        cycle_shifts,
        kernel,
        fragment_bins,
    )

    coarse = pl.pallas_call(
        coarse_kernel,
        out_shape=jax.ShapeDtypeStruct((gas_cycles, 3 * cells), F32),
        name="coarse",
    )(gas_density, gas_flat)
    prev = shifted(coarse, "rad", 1)

    coag = coag.reshape(cycles * cells, bins)
    vel_out, back, kick = pl.pallas_call(
        drag_kernel,
        out_shape=(
            jax.ShapeDtypeStruct((2 * cycles * cells, bins), F32),
            jax.ShapeDtypeStruct((2 * cells, gas_cycles), F32),
            jax.ShapeDtypeStruct((2 * cells, gas_cycles), F32),
        ),
        compiler_params=pltpu.CompilerParams(vmem_limit_bytes=32 * 2**20),
        name="drag",
    )(
        gas_map.reshape(1, cycles),
        prev,
        coarse,
        grain_param.reshape(1, bins),
        coag,
        vel.reshape(2 * cycles * cells, bins),
    )
    from_next = shifted(back, "rad", -1)
    gas_out = pl.pallas_call(
        gas_kernel,
        out_shape=jax.ShapeDtypeStruct((gas_cycles, 2 * fine), F32),
        name="gas",
    )(kick, from_next, gas_density, gas_flat)
    return (
        coag.reshape(cycles, cells, bins),
        vel_out.reshape(cycles, cells, 2, bins),
        gas_out.reshape(gas_cycles, 2, fine),
    )


def solution(mesh):
    placed = (
        P("rad", "az", None),
        P("rad", "az", None, None),
        P("rad", "az"),
        P("rad", None, "az"),
        P(),
        P(),
        P("rad"),
        P(),
        P("rad"),
    )
    return jax.shard_map(
        body,
        mesh=mesh,
        in_specs=placed,
        out_specs=(P("rad", "az", None), P("rad", "az", None, None), P("rad", None, "az")),
        check_vma=False,
    )
```

```python
import functools

import jax
import jax.numpy as jnp
from jax import lax
from jax.experimental import pallas as pl
from jax.experimental.pallas import tpu as pltpu
from jax.sharding import PartitionSpec as P

F32 = jnp.float32
BF16 = jnp.bfloat16
VMEM = pl.BlockSpec(memory_space=pltpu.VMEM)
SMEM = pl.BlockSpec(memory_space=pltpu.SMEM)
GROUP = 6
ABT = (((1,), (1,)), ((), ()))


def split_parts(x):
    hi = x.astype(BF16)
    return hi, (x - hi.astype(F32)).astype(BF16)


def diagonals(x):
    n = x.shape[0]
    lane = lax.broadcasted_iota(jnp.int32, x.shape, 1)
    step = 1
    while step < n:
        x = jnp.where((lane & step) != 0, pltpu.roll(x, n - step, 0), x)
        step *= 2
    return x


def coagulate(dens_ref, rate_ref, bins_ref, out_ref, rates, places, acc):
    n = rate_ref.shape[0]
    half = n // 2
    rate = rate_ref[...]
    place = bins_ref[...].astype(F32)
    dist = lax.broadcasted_iota(jnp.int32, (n, n), 0)
    rates[0] = jnp.where(dist <= half, diagonals(rate.T), 0.0)
    rates[1] = jnp.where((dist > 0) & (dist < half), diagonals(rate), 0.0)
    places[0] = diagonals(place.T)
    places[1] = diagonals(place)

    dens = dens_ref[...]
    hi, lo = split_parts(dens)
    rate_hi, rate_lo = split_parts(rate)
    both = jnp.concatenate([rate_hi, rate_lo], axis=0)
    lost = lax.dot_general(
        jnp.concatenate([hi, lo], axis=1),
        jnp.concatenate([both, both], axis=1),
        ABT,
        preferred_element_type=F32,
    )
    out_ref[...] = dens - dens * (lost[:, :n] + lost[:, n:])
    acc[...] = jnp.zeros_like(acc)
    bin_id = lax.broadcasted_iota(jnp.int32, (n, n), 0).astype(F32)

    def step(g, carry):
        table_hi, table_lo, pair_hi, pair_lo = [], [], [], []
        for t in range(GROUP):
            d = g * GROUP + t
            row = pl.ds(d, 1)
            table = jnp.where(bin_id == places[0, row, :], rates[0, row, :], 0.0) + jnp.where(
                bin_id == places[1, row, :], rates[1, row, :], 0.0
            )
            h, l = split_parts(table)
            table_hi.append(h)
            table_lo.append(l)
            x = dens_ref[...]
            h, l = split_parts(x * pltpu.roll(x, n - d, 1))
            pair_hi.append(h)
            pair_lo.append(l)
        table = jnp.concatenate(
            [jnp.concatenate(table_hi, axis=1), jnp.concatenate(table_lo, axis=1)], axis=0
        )
        acc[...] += lax.dot_general(
            jnp.concatenate(pair_hi, axis=1), table, ABT, preferred_element_type=F32
        ) + lax.dot_general(
            jnp.concatenate(pair_lo, axis=1), table, ABT, preferred_element_type=F32
        )
        return carry

    lax.fori_loop(0, -(-(half + 1) // GROUP), step, 0)
    out_ref[...] += acc[:, :n] + acc[:, n:]


def beside(axis):
    n = lax.axis_size(axis)
    me = lax.axis_index(axis)
    return lax.rem(me + n - 1, n), lax.rem(me + 1, n)


def coarsen(dens_ref, vel_ref, out_ref):
    fine = dens_ref.shape[1]
    cells = fine // 4
    q = lax.broadcasted_iota(jnp.int32, (fine, cells), 0)
    p = lax.broadcasted_iota(jnp.int32, (fine, cells), 1)
    pool = jnp.where((q >= 4 * p) & (q < 4 * p + 4), 0.25, 0.0)
    vel = vel_ref[...]
    parts = [dens_ref[...], vel[:, :fine], vel[:, fine:]]
    for i, x in enumerate(parts):
        out_ref[:, i * cells : (i + 1) * cells] = jnp.dot(
            x, pool, precision=lax.Precision.HIGHEST, preferred_element_type=F32
        )


def move_kernel(
    owned, shifts_ref, vel_ref, start_ref, rate_ref, bins_ref, gas_dens_ref, gas_vel_ref,
    vel_out, dens_out, coarse_ref, prev_ref,
    flat, dens_ref, rates, places, acc, vel_land, dens_land, vel_turned, dens_turned, vel_twice, dens_twice, send_sem, recv_sem, gas_sem,
):
    me = lax.axis_index("az")
    parts = vel_ref.shape[0]
    half = owned // 2
    vel = (vel_ref, vel_land, vel_turned, vel_out, vel_twice, 2)
    dens = (dens_ref, dens_land, dens_turned, dens_out, dens_twice, 1)
    units = [vel + (0, half), vel + (half, owned - half), dens + (0, owned)]

    barrier = pltpu.get_barrier_semaphore()

    def greet(k, carry):
        other = lax.rem(me + k, parts)
        pl.semaphore_signal(
            barrier, inc=1, device_id={"az": other}, device_id_type=pl.DeviceIdType.MESH
        )
        return carry

    lax.fori_loop(1, parts, greet, 0)
    before, after = beside("rad")
    pl.semaphore_signal(
        barrier, inc=1, device_id={"rad": before}, device_id_type=pl.DeviceIdType.MESH
    )
    pl.semaphore_wait(barrier, parts)
    onward = pltpu.make_async_remote_copy(
        src_ref=coarse_ref,
        dst_ref=prev_ref,
        send_sem=gas_sem.at[0],
        recv_sem=gas_sem.at[1],
        device_id={"rad": after},
        device_id_type=pl.DeviceIdType.MESH,
    )

    def copy(phase, u, k):
        source, land, turned, end, _, _, first, count = units[u]
        src, dst = (source, land) if phase == 0 else (turned, end)
        other = lax.rem(me + k, parts)
        own = pl.ds(first, count)
        return pltpu.make_async_remote_copy(
            src_ref=src.at[other, own],
            dst_ref=dst.at[me, own],
            send_sem=send_sem.at[phase, u, k],
            recv_sem=recv_sem.at[phase, u, k],
            device_id={"az": other},
            device_id_type=pl.DeviceIdType.MESH,
        )

    def each(act):
        def step(k, carry):
            act(k)
            return carry

        lax.fori_loop(1, parts, step, 0)

    for u, (source, land, _, _, _, _, first, count) in enumerate(units):
        if source is dens_ref:
            coarsen(gas_dens_ref, gas_vel_ref, coarse_ref)
            onward.start()
            coagulate(start_ref, rate_ref, bins_ref, flat, rates, places, acc)
            dens_ref[...] = flat[...].reshape(dens_ref.shape)
        each(lambda k: copy(0, u, k).start())
        land[me, pl.ds(first, count)] = source[me, pl.ds(first, count)]

    for u, (_, land, turned, end, twice, per_cell, first, count) in enumerate(units):
        each(lambda k: copy(0, u, k).wait_recv())
        rows, n = land.shape[2:]
        whole = parts * rows
        for c in range(first, first + count):
            x = land[:, c].reshape(whole, n)
            twice[c, :whole] = x
            twice[c, whole:] = x
            shift = shifts_ref[me * owned + c] * per_cell
            turned[:, c] = twice[c, pl.ds(whole - shift, whole), :].reshape(parts, rows, n)
        each(lambda k: copy(1, u, k).start())
        end[me, pl.ds(first, count)] = turned[me, pl.ds(first, count)]

    for u in range(len(units)):
        each(lambda k: copy(1, u, k).wait_recv())
    for phase in range(2):
        for u in range(len(units)):
            each(lambda k: copy(phase, u, k).wait_send())
    onward.wait()


def move(vel, dens, shifts, kernel, fragment_bins, gas_density, gas_flat):
    parts, owned, rows, n = vel.shape
    cells = rows // 2
    moved = (parts, owned, cells, n)
    coarse = jax.ShapeDtypeStruct((gas_density.shape[0], 3 * cells), F32)
    return pl.pallas_call(
        functools.partial(move_kernel, owned),
        out_shape=(
            jax.ShapeDtypeStruct(vel.shape, F32),
            jax.ShapeDtypeStruct(moved, F32),
            coarse,
            coarse,
        ),
        in_specs=[SMEM] + [VMEM] * 6,
        out_specs=(VMEM,) * 4,
        scratch_shapes=[
            pltpu.VMEM(dens.shape, F32),
            pltpu.VMEM(moved, F32),
            pltpu.VMEM((2, n, n), F32),
            pltpu.VMEM((2, n, n), F32),
            pltpu.VMEM((dens.shape[0], 2 * n), F32),
            pltpu.VMEM(vel.shape, F32),
            pltpu.VMEM(moved, F32),
            pltpu.VMEM(vel.shape, F32),
            pltpu.VMEM(moved, F32),
            pltpu.VMEM((owned, 2 * parts * rows, n), F32),
            pltpu.VMEM((owned, 2 * parts * cells, n), F32),
            pltpu.SemaphoreType.DMA((2, 3, parts)),
            pltpu.SemaphoreType.DMA((2, 3, parts)),
            pltpu.SemaphoreType.DMA((2,)),
        ],
        compiler_params=pltpu.CompilerParams(
            collective_id=0, has_side_effects=True, vmem_limit_bytes=48 * 2**20
        ),
        cost_estimate=pl.CostEstimate(
            flops=4 * dens.size * n * n,
            bytes_accessed=8 * (vel.size + dens.size),
            transcendentals=0,
        ),
        name="move",
    )(shifts, vel, dens, kernel, fragment_bins, gas_density, gas_flat)


def drag_kernel(
    map_ref, prev_ref, own_ref, grain_ref, coag_ref, vel_ref, vel_out_ref, back_ref, kick_ref
):
    cycles = map_ref.shape[1]
    gas_cycles = own_ref.shape[0]
    cells = own_ref.shape[1] // 3
    n = grain_ref.shape[1]
    first = (lax.axis_index("rad") - 1) * gas_cycles
    row = lax.broadcasted_iota(jnp.int32, (2 * gas_cycles, cycles), 0)
    select = jnp.where(map_ref[...] - first == row, 1.0, 0.0)
    near = jnp.concatenate([prev_ref[...], own_ref[...]], axis=0)
    gas = lax.dot_general(
        near.T, select, (((1,), (0,)), ((), ())),
        precision=lax.Precision.HIGHEST, preferred_element_type=F32,
    )
    grain = grain_ref[...]
    lane = lax.broadcasted_iota(jnp.int32, (cells, cycles), 1)
    moment = [jnp.zeros((cells, cycles), F32) for _ in range(2)]
    for r in range(cycles):
        rho = gas[:cells, r : r + 1]
        frac = 1.0 - jnp.exp(-rho / grain)
        dens = coag_ref[r * cells : (r + 1) * cells, :]
        for c in range(2):
            u = gas[(c + 1) * cells : (c + 2) * cells, r : r + 1]
            rows = pl.ds(r * 2 * cells + c, cells, 2)
            v = vel_ref[rows, :]
            new = v + (u - v) * frac
            vel_out_ref[rows, :] = new
            m = jnp.sum(dens * (new - v), axis=1, keepdims=True)
            moment[c] = jnp.where(lane == r, m, moment[c])
    both = jnp.concatenate(moment, axis=0) / n
    kick = lax.dot_general(
        both, select, ABT, precision=lax.Precision.HIGHEST, preferred_element_type=F32
    )
    back_ref[...] = kick[:, :gas_cycles]
    kick_ref[...] = kick[:, gas_cycles:]


def gas_kernel(kick_ref, back_ref, dens_ref, vel_ref, out_ref, from_next_ref, sems):
    before, after = beside("rad")
    barrier = pltpu.get_barrier_semaphore()
    pl.semaphore_signal(
        barrier, inc=1, device_id={"rad": after}, device_id_type=pl.DeviceIdType.MESH
    )
    pl.semaphore_wait(barrier, 1)
    back = pltpu.make_async_remote_copy(
        src_ref=back_ref,
        dst_ref=from_next_ref,
        send_sem=sems.at[0],
        recv_sem=sems.at[1],
        device_id={"rad": before},
        device_id_type=pl.DeviceIdType.MESH,
    )
    back.start()
    back.wait()
    fine = dens_ref.shape[1]
    cells = fine // 4
    kick = (kick_ref[...] + from_next_ref[...]).T
    p = lax.broadcasted_iota(jnp.int32, (cells, fine), 0)
    q = lax.broadcasted_iota(jnp.int32, (cells, fine), 1)
    spread = jnp.where((q >= 4 * p) & (q < 4 * p + 4), 1.0, 0.0)
    dens = dens_ref[...]
    for c in range(2):
        wide = jnp.dot(
            kick[:, c * cells : (c + 1) * cells], spread,
            precision=lax.Precision.HIGHEST, preferred_element_type=F32,
        )
        own = slice(c * fine, (c + 1) * fine)
        out_ref[:, own] = vel_ref[:, own] - wide / dens


def body(
    dust_density,
    dust_velocity,
    gas_density,
    gas_velocity,
    kernel,
    grain_param,
    cycle_shifts,
    fragment_bins,
    gas_map,
):
    cycles, cells, bins = dust_density.shape
    gas_cycles, fine = gas_density.shape
    parts = lax.axis_size("az")
    owned = cycles // parts
    gas_flat = gas_velocity.reshape(gas_cycles, 2 * fine)

    vel, coag, coarse, prev = move(
        dust_velocity.reshape(parts, owned, 2 * cells, bins),
        dust_density.reshape(cycles * cells, bins),
        cycle_shifts,
        kernel,
        fragment_bins,
        gas_density,
        gas_flat,
    )

    coag = coag.reshape(cycles * cells, bins)
    vel_out, back, kick = pl.pallas_call(
        drag_kernel,
        out_shape=(
            jax.ShapeDtypeStruct((2 * cycles * cells, bins), F32),
            jax.ShapeDtypeStruct((2 * cells, gas_cycles), F32),
            jax.ShapeDtypeStruct((2 * cells, gas_cycles), F32),
        ),
        compiler_params=pltpu.CompilerParams(vmem_limit_bytes=32 * 2**20),
        name="drag",
    )(
        gas_map.reshape(1, cycles),
        prev,
        coarse,
        grain_param.reshape(1, bins),
        coag,
        vel.reshape(2 * cycles * cells, bins),
    )
    gas_out = pl.pallas_call(
        gas_kernel,
        out_shape=jax.ShapeDtypeStruct((gas_cycles, 2 * fine), F32),
        in_specs=[VMEM] * 4,
        out_specs=VMEM,
        scratch_shapes=[
            pltpu.VMEM((2 * cells, gas_cycles), F32),
            pltpu.SemaphoreType.DMA((2,)),
        ],
        compiler_params=pltpu.CompilerParams(collective_id=1, has_side_effects=True),
        name="gas",
    )(kick, back, gas_density, gas_flat)
    return (
        coag.reshape(cycles, cells, bins),
        vel_out.reshape(cycles, cells, 2, bins),
        gas_out.reshape(gas_cycles, 2, fine),
    )


def solution(mesh):
    placed = (
        P("rad", "az", None),
        P("rad", "az", None, None),
        P("rad", "az"),
        P("rad", None, "az"),
        P(),
        P(),
        P("rad"),
        P(),
        P("rad"),
    )
    return jax.shard_map(
        body,
        mesh=mesh,
        in_specs=placed,
        out_specs=(P("rad", "az", None), P("rad", "az", None, None), P("rad", None, "az")),
        check_vma=False,
    )
```

```python
import functools
import math

import jax
import jax.numpy as jnp
from jax import lax
from jax.experimental import pallas as pl
from jax.experimental.pallas import tpu as pltpu
from jax.sharding import PartitionSpec as P

F32 = jnp.float32
BF16 = jnp.bfloat16
VMEM = pl.BlockSpec(memory_space=pltpu.VMEM)
SMEM = pl.BlockSpec(memory_space=pltpu.SMEM)
GROUP = 6
ABT = (((1,), (1,)), ((), ()))


def split_parts(x):
    hi = x.astype(BF16)
    return hi, (x - hi.astype(F32)).astype(BF16)


def diagonals(x):
    n = x.shape[0]
    lane = lax.broadcasted_iota(jnp.int32, x.shape, 1)
    step = 1
    while step < n:
        x = jnp.where((lane & step) != 0, pltpu.roll(x, n - step, 0), x)
        step *= 2
    return x


def coagulate(dens_ref, rate_ref, bins_ref, out_ref, rates, places, acc):
    n = rate_ref.shape[0]
    half = n // 2
    rate = rate_ref[...]
    place = bins_ref[...].astype(F32)
    dist = lax.broadcasted_iota(jnp.int32, (n, n), 0)
    rates[0] = jnp.where(dist <= half, diagonals(rate.T), 0.0)
    rates[1] = jnp.where((dist > 0) & (dist < half), diagonals(rate), 0.0)
    places[0] = diagonals(place.T)
    places[1] = diagonals(place)

    dens = dens_ref[...]
    hi, lo = split_parts(dens)
    rate_hi, rate_lo = split_parts(rate)
    both = jnp.concatenate([rate_hi, rate_lo], axis=0)
    lost = lax.dot_general(
        jnp.concatenate([hi, lo], axis=1),
        jnp.concatenate([both, both], axis=1),
        ABT,
        preferred_element_type=F32,
    )
    out_ref[...] = dens - dens * (lost[:, :n] + lost[:, n:])
    acc[...] = jnp.zeros_like(acc)
    bin_id = lax.broadcasted_iota(jnp.int32, (n, n), 0).astype(F32)

    def step(g, carry):
        table_hi, table_lo, pair_hi, pair_lo = [], [], [], []
        for t in range(GROUP):
            d = g * GROUP + t
            row = pl.ds(d, 1)
            table = jnp.where(bin_id == places[0, row, :], rates[0, row, :], 0.0) + jnp.where(
                bin_id == places[1, row, :], rates[1, row, :], 0.0
            )
            h, l = split_parts(table)
            table_hi.append(h)
            table_lo.append(l)
            x = dens_ref[...]
            h, l = split_parts(x * pltpu.roll(x, n - d, 1))
            pair_hi.append(h)
            pair_lo.append(l)
        table = jnp.concatenate(
            [jnp.concatenate(table_hi, axis=1), jnp.concatenate(table_lo, axis=1)], axis=0
        )
        acc[...] += lax.dot_general(
            jnp.concatenate(pair_hi, axis=1), table, ABT, preferred_element_type=F32
        ) + lax.dot_general(
            jnp.concatenate(pair_lo, axis=1), table, ABT, preferred_element_type=F32
        )
        return carry

    lax.fori_loop(0, -(-(half + 1) // GROUP), step, 0)
    out_ref[...] += acc[:, :n] + acc[:, n:]


def beside(axis):
    n = lax.axis_size(axis)
    me = lax.axis_index(axis)
    return lax.rem(me + n - 1, n), lax.rem(me + 1, n)


def coarsen(dens_ref, vel_ref, out_ref):
    fine = dens_ref.shape[1]
    cells = fine // 4
    q = lax.broadcasted_iota(jnp.int32, (fine, cells), 0)
    p = lax.broadcasted_iota(jnp.int32, (fine, cells), 1)
    pool = jnp.where((q >= 4 * p) & (q < 4 * p + 4), 0.25, 0.0)
    vel = vel_ref[...]
    parts = [dens_ref[...], vel[:, :fine], vel[:, fine:]]
    for i, x in enumerate(parts):
        out_ref[:, i * cells : (i + 1) * cells] = jnp.dot(
            x, pool, precision=lax.Precision.HIGHEST, preferred_element_type=F32
        )


def move_kernel(
    owned, shifts_ref, vel_ref, start_ref, rate_ref, bins_ref, gas_dens_ref, gas_vel_ref,
    vel_out, dens_out, coarse_ref, prev_ref,
    flat, dens_ref, rates, places, acc, vel_land, dens_land, vel_turned, dens_turned, vel_twice, dens_twice, send_sem, recv_sem, gas_sem,
):
    me = lax.axis_index("az")
    parts = vel_ref.shape[0]
    half = owned // 2
    vel = (vel_ref, vel_land, vel_turned, vel_out, vel_twice, 2)
    dens = (dens_ref, dens_land, dens_turned, dens_out, dens_twice, 1)
    units = [vel + (0, half), vel + (half, owned - half), dens + (0, owned)]

    barrier = pltpu.get_barrier_semaphore()

    def greet(k, carry):
        other = lax.rem(me + k, parts)
        pl.semaphore_signal(
            barrier, inc=1, device_id={"az": other}, device_id_type=pl.DeviceIdType.MESH
        )
        return carry

    lax.fori_loop(1, parts, greet, 0)
    before, after = beside("rad")
    pl.semaphore_signal(
        barrier, inc=1, device_id={"rad": before}, device_id_type=pl.DeviceIdType.MESH
    )
    pl.semaphore_wait(barrier, parts)
    onward = pltpu.make_async_remote_copy(
        src_ref=coarse_ref,
        dst_ref=prev_ref,
        send_sem=gas_sem.at[0],
        recv_sem=gas_sem.at[1],
        device_id={"rad": after},
        device_id_type=pl.DeviceIdType.MESH,
    )

    def copy(phase, u, k):
        source, land, turned, end, _, _, first, count = units[u]
        src, dst = (source, land) if phase == 0 else (turned, end)
        other = lax.rem(me + k, parts)
        own = pl.ds(first, count)
        return pltpu.make_async_remote_copy(
            src_ref=src.at[other, own],
            dst_ref=dst.at[me, own],
            send_sem=send_sem.at[phase, u, k],
            recv_sem=recv_sem.at[phase, u, k],
            device_id={"az": other},
            device_id_type=pl.DeviceIdType.MESH,
        )

    stride = next(m for m in range(max(parts // 2 - 1, 1), parts) if math.gcd(m, parts - 1) == 1)

    def each(act):
        def step(k, carry):
            act(1 + lax.rem((k - 1) * stride, parts - 1))
            return carry

        lax.fori_loop(1, parts, step, 0)

    for u, (source, land, _, _, _, _, first, count) in enumerate(units):
        if source is dens_ref:
            coarsen(gas_dens_ref, gas_vel_ref, coarse_ref)
            onward.start()
            coagulate(start_ref, rate_ref, bins_ref, flat, rates, places, acc)
            dens_ref[...] = flat[...].reshape(dens_ref.shape)
        each(lambda k: copy(0, u, k).start())
        land[me, pl.ds(first, count)] = source[me, pl.ds(first, count)]

    for u, (_, land, turned, end, twice, per_cell, first, count) in enumerate(units):
        each(lambda k: copy(0, u, k).wait_recv())
        rows, n = land.shape[2:]
        whole = parts * rows
        for c in range(first, first + count):
            x = land[:, c].reshape(whole, n)
            twice[c, :whole] = x
            twice[c, whole:] = x
            shift = shifts_ref[me * owned + c] * per_cell
            turned[:, c] = twice[c, pl.ds(whole - shift, whole), :].reshape(parts, rows, n)
        each(lambda k: copy(1, u, k).start())
        end[me, pl.ds(first, count)] = turned[me, pl.ds(first, count)]

    for u in range(len(units)):
        each(lambda k: copy(1, u, k).wait_recv())
    for phase in range(2):
        for u in range(len(units)):
            each(lambda k: copy(phase, u, k).wait_send())
    onward.wait()


def move(vel, dens, shifts, kernel, fragment_bins, gas_density, gas_flat):
    parts, owned, rows, n = vel.shape
    cells = rows // 2
    moved = (parts, owned, cells, n)
    coarse = jax.ShapeDtypeStruct((gas_density.shape[0], 3 * cells), F32)
    return pl.pallas_call(
        functools.partial(move_kernel, owned),
        out_shape=(
            jax.ShapeDtypeStruct(vel.shape, F32),
            jax.ShapeDtypeStruct(moved, F32),
            coarse,
            coarse,
        ),
        in_specs=[SMEM] + [VMEM] * 6,
        out_specs=(VMEM,) * 4,
        scratch_shapes=[
            pltpu.VMEM(dens.shape, F32),
            pltpu.VMEM(moved, F32),
            pltpu.VMEM((2, n, n), F32),
            pltpu.VMEM((2, n, n), F32),
            pltpu.VMEM((dens.shape[0], 2 * n), F32),
            pltpu.VMEM(vel.shape, F32),
            pltpu.VMEM(moved, F32),
            pltpu.VMEM(vel.shape, F32),
            pltpu.VMEM(moved, F32),
            pltpu.VMEM((owned, 2 * parts * rows, n), F32),
            pltpu.VMEM((owned, 2 * parts * cells, n), F32),
            pltpu.SemaphoreType.DMA((2, 3, parts)),
            pltpu.SemaphoreType.DMA((2, 3, parts)),
            pltpu.SemaphoreType.DMA((2,)),
        ],
        compiler_params=pltpu.CompilerParams(
            collective_id=0, has_side_effects=True, vmem_limit_bytes=48 * 2**20
        ),
        cost_estimate=pl.CostEstimate(
            flops=4 * dens.size * n * n,
            bytes_accessed=8 * (vel.size + dens.size),
            transcendentals=0,
        ),
        name="move",
    )(shifts, vel, dens, kernel, fragment_bins, gas_density, gas_flat)


def drag_kernel(
    map_ref, prev_ref, own_ref, grain_ref, coag_ref, vel_ref, vel_out_ref, back_ref, kick_ref
):
    cycles = map_ref.shape[1]
    gas_cycles = own_ref.shape[0]
    cells = own_ref.shape[1] // 3
    n = grain_ref.shape[1]
    first = (lax.axis_index("rad") - 1) * gas_cycles
    row = lax.broadcasted_iota(jnp.int32, (2 * gas_cycles, cycles), 0)
    select = jnp.where(map_ref[...] - first == row, 1.0, 0.0)
    near = jnp.concatenate([prev_ref[...], own_ref[...]], axis=0)
    gas = lax.dot_general(
        near.T, select, (((1,), (0,)), ((), ())),
        precision=lax.Precision.HIGHEST, preferred_element_type=F32,
    )
    grain = grain_ref[...]
    lane = lax.broadcasted_iota(jnp.int32, (cells, cycles), 1)
    moment = [jnp.zeros((cells, cycles), F32) for _ in range(2)]
    for r in range(cycles):
        rho = gas[:cells, r : r + 1]
        frac = 1.0 - jnp.exp(-rho / grain)
        dens = coag_ref[r * cells : (r + 1) * cells, :]
        for c in range(2):
            u = gas[(c + 1) * cells : (c + 2) * cells, r : r + 1]
            rows = pl.ds(r * 2 * cells + c, cells, 2)
            v = vel_ref[rows, :]
            new = v + (u - v) * frac
            vel_out_ref[rows, :] = new
            m = jnp.sum(dens * (new - v), axis=1, keepdims=True)
            moment[c] = jnp.where(lane == r, m, moment[c])
    both = jnp.concatenate(moment, axis=0) / n
    kick = lax.dot_general(
        both, select, ABT, precision=lax.Precision.HIGHEST, preferred_element_type=F32
    )
    back_ref[...] = kick[:, :gas_cycles]
    kick_ref[...] = kick[:, gas_cycles:]


def gas_kernel(kick_ref, back_ref, dens_ref, vel_ref, out_ref, from_next_ref, sems):
    before, after = beside("rad")
    barrier = pltpu.get_barrier_semaphore()
    pl.semaphore_signal(
        barrier, inc=1, device_id={"rad": after}, device_id_type=pl.DeviceIdType.MESH
    )
    pl.semaphore_wait(barrier, 1)
    back = pltpu.make_async_remote_copy(
        src_ref=back_ref,
        dst_ref=from_next_ref,
        send_sem=sems.at[0],
        recv_sem=sems.at[1],
        device_id={"rad": before},
        device_id_type=pl.DeviceIdType.MESH,
    )
    back.start()
    back.wait()
    fine = dens_ref.shape[1]
    cells = fine // 4
    kick = (kick_ref[...] + from_next_ref[...]).T
    p = lax.broadcasted_iota(jnp.int32, (cells, fine), 0)
    q = lax.broadcasted_iota(jnp.int32, (cells, fine), 1)
    spread = jnp.where((q >= 4 * p) & (q < 4 * p + 4), 1.0, 0.0)
    dens = dens_ref[...]
    for c in range(2):
        wide = jnp.dot(
            kick[:, c * cells : (c + 1) * cells], spread,
            precision=lax.Precision.HIGHEST, preferred_element_type=F32,
        )
        own = slice(c * fine, (c + 1) * fine)
        out_ref[:, own] = vel_ref[:, own] - wide / dens


def body(
    dust_density,
    dust_velocity,
    gas_density,
    gas_velocity,
    kernel,
    grain_param,
    cycle_shifts,
    fragment_bins,
    gas_map,
):
    cycles, cells, bins = dust_density.shape
    gas_cycles, fine = gas_density.shape
    parts = lax.axis_size("az")
    owned = cycles // parts
    gas_flat = gas_velocity.reshape(gas_cycles, 2 * fine)

    vel, coag, coarse, prev = move(
        dust_velocity.reshape(parts, owned, 2 * cells, bins),
        dust_density.reshape(cycles * cells, bins),
        cycle_shifts,
        kernel,
        fragment_bins,
        gas_density,
        gas_flat,
    )

    coag = coag.reshape(cycles * cells, bins)
    vel_out, back, kick = pl.pallas_call(
        drag_kernel,
        out_shape=(
            jax.ShapeDtypeStruct((2 * cycles * cells, bins), F32),
            jax.ShapeDtypeStruct((2 * cells, gas_cycles), F32),
            jax.ShapeDtypeStruct((2 * cells, gas_cycles), F32),
        ),
        compiler_params=pltpu.CompilerParams(vmem_limit_bytes=32 * 2**20),
        name="drag",
    )(
        gas_map.reshape(1, cycles),
        prev,
        coarse,
        grain_param.reshape(1, bins),
        coag,
        vel.reshape(2 * cycles * cells, bins),
    )
    gas_out = pl.pallas_call(
        gas_kernel,
        out_shape=jax.ShapeDtypeStruct((gas_cycles, 2 * fine), F32),
        in_specs=[VMEM] * 4,
        out_specs=VMEM,
        scratch_shapes=[
            pltpu.VMEM((2 * cells, gas_cycles), F32),
            pltpu.SemaphoreType.DMA((2,)),
        ],
        compiler_params=pltpu.CompilerParams(collective_id=1, has_side_effects=True),
        name="gas",
    )(kick, back, gas_density, gas_flat)
    return (
        coag.reshape(cycles, cells, bins),
        vel_out.reshape(cycles, cells, 2, bins),
        gas_out.reshape(gas_cycles, 2, fine),
    )


def solution(mesh):
    placed = (
        P("rad", "az", None),
        P("rad", "az", None, None),
        P("rad", "az"),
        P("rad", None, "az"),
        P(),
        P(),
        P("rad"),
        P(),
        P("rad"),
    )
    return jax.shard_map(
        body,
        mesh=mesh,
        in_specs=placed,
        out_specs=(P("rad", "az", None), P("rad", "az", None, None), P("rad", None, "az")),
        check_vma=False,
    )
```
